32 devices in a mesh: rep: 2 (over y), steal: 4 (over x, core), ep: 4 (over z).
Axes of the slice: x: 2, y: 2, z: 4, core: 2. Of those that a mesh axis runs over, the one named last changes fastest.
Arguments:
- queries: bfloat16 [512, 128, 576], P(('rep', 'steal', 'ep')), parts along dimension 0
- latent_cache: bfloat16 [512, 128, 576], P(('rep', 'steal', 'ep')), parts along dimension 0
- cache_length: int32 [512], P(('rep', 'steal', 'ep')), parts along dimension 0, may hold values from 16 to 128, as said below
- steal_source: int32 [512], P(('rep', 'steal', 'ep')), parts along dimension 0, may hold values from 0 to 3, as said below
- hidden: bfloat16 [512, 7168], P(('rep', 'steal', 'ep')), parts along dimension 0
- norm_gain: float32 [7168], replicated, may hold values from 0.1 to 1.9
- expert_ids: int32 [512, 2], P(('rep', 'steal', 'ep')), parts along dimension 0, may hold values from 0 to 3, all different within a row; in each aligned block of 16 rows (0 to 15, 16 to 31, ...) at most 12 rows name the same one
- expert_weight: float32 [512, 2], P(('rep', 'steal', 'ep')), parts along dimension 0, may hold values from 0.05 to 0.45
- w_gate: bfloat16 [4, 7168, 1024], P('ep', 'steal'), may hold values from -0.0625 to 0.0625
- w_up: bfloat16 [4, 7168, 1024], P('ep', 'steal'), may hold values from -0.0625 to 0.0625
- w_down: bfloat16 [4, 1024, 7168], P('ep', None, 'steal'), may hold values from -0.1875 to 0.1875
Outputs:
- attended: bfloat16 [512, 128, 512], P(('rep', 'steal', 'ep')), parts along dimension 0
- mixed: bfloat16 [512, 7168], P(('rep', 'steal', 'ep')), parts along dimension 0
The draws below stay inside these ranges and needn't reach their ends.
There are 2 independent parts, one for each index of `rep`. The reference program is written for one: setup_inputs(seed, part) draws one part's arguments, and reference() takes and returns one part's arrays. A program takes and returns all parts, laid end to end along the dimension named above; an argument that names none is the same for every part. Nothing has to cross between parts.
Inputs may be any that keep to these rules, and one draw needn't show every extreme that they name: Slots 3 and later of every device serve the device's own request (steal_source equals the device's steal index). For a slot j below 3 and one ep index, all devices along steal share one offset o in 1 to 3 with steal_source = (steal index - o) mod 4, and the 3 slots of an ep index have distinct offsets. `cache_length`: every device serves a request with exactly 128 valid positions. `expert_ids`: the rows of one device name one expert at most 12 times.
All inputs are finite; a program needn't handle non-finite values.
Results may differ from the reference program's by a relative error of at most 0.019.
Values may be sent and summed in bfloat16 or wider, within the bound.
No kernel may reach another device: no remote copies, remote signals or barrier semaphores. Data moves between devices by JAX's collectives and lax.ppermute only.
A program may use at most 128 MiB of HBM per device.

```python
import math
import jax
import jax.numpy as jnp
import numpy as np
from jax import lax

D = 7168
HEADS = 128
LAT = 512
ROPE = 64
FF = 1024
REQ = 16
CAP = 128
EXPERTS = 4
TOP = 2
ROWS = 256
CAP_E = 12
N_STEAL = 4
N_EP = 4


def shared_cache(key):
    return jnp.clip(jax.random.normal(key, (ROWS, CAP, LAT + ROPE), jnp.float32), -6.0, 6.0)


def draw_latent_cache(key, part):
    base = shared_cache(key)
    return base.astype(jnp.bfloat16)


def draw_queries(key, part):
    key = jax.random.fold_in(key, 7)
    query = jnp.clip(0.6 * jax.random.normal(key, (ROWS, HEADS, LAT + ROPE), jnp.float32), -3.6, 3.6)
    return query.astype(jnp.bfloat16)


def draw_cache_length(key, part):
    key = jax.random.fold_in(key, 3)
    low_key, len_key, full_key = jax.random.split(key, 3)
    devices = ROWS // REQ
    floor_dev = jax.random.randint(low_key, (devices, 1), CAP // 8, CAP // 2 + 1)
    base = jax.random.randint(len_key, (devices, REQ), 0, CAP + 1)
    lengths = floor_dev + base % (CAP + 1 - floor_dev)
    full_slot = jax.random.randint(full_key, (devices, 1), 0, REQ)
    lengths = jnp.where(jnp.arange(REQ)[None, :] == full_slot, CAP, lengths)
    return lengths.reshape(-1).astype(jnp.int32)


def draw_steal_source(key, part):
    key = jax.random.fold_in(key, 5)
    raw = jax.random.randint(key, (N_EP, N_STEAL - 1), 0, 1 << 20)
    order = jnp.argsort(raw * N_STEAL + jnp.arange(N_STEAL - 1)[None, :], axis=1)
    offsets = (order + 1).astype(jnp.int32)
    steal_idx = jnp.arange(N_STEAL, dtype=jnp.int32)[:, None, None]
    lent = (steal_idx - offsets[None, :, :]) % N_STEAL
    kept = jnp.broadcast_to(steal_idx, (N_STEAL, N_EP, REQ - N_STEAL + 1))
    return jnp.concatenate([lent, kept], axis=-1).reshape(-1).astype(jnp.int32)


def draw_hidden(key, part):
    key = jax.random.fold_in(key, 9)
    base_key, row_key, col_key = jax.random.split(key, 3)
    base = jnp.clip(jax.random.normal(base_key, (ROWS, D), jnp.float32), -6.0, 6.0)
    row_scale = jnp.exp(jax.random.uniform(row_key, (ROWS, 1), jnp.float32, 0.0, 2.31))
    col_scale = jnp.exp(jax.random.uniform(col_key, (1, D), jnp.float32, -0.69, 0.69))
    return (base * row_scale * col_scale).astype(jnp.bfloat16)


def level_of(stream_key, shape, cuts, least, largest):
    gain = 1.0
    for axis_at, blocks in cuts:
        steps = jax.random.uniform(jax.random.fold_in(jax.random.fold_in(stream_key, 6), axis_at), (blocks,), jnp.float32, least / len(cuts), largest / len(cuts))
        gain = gain * jnp.repeat(jnp.exp(steps), shape[axis_at] // blocks).reshape((-1,) + (1,) * (len(shape) - 1 - axis_at))
    return gain


def assign_block(key, own, number, rows, amount, top, bound, skew):
    sequence = jax.random.permutation(key, amount)
    heavy_load, common = shares(amount, rows * top, bound, skew, True), shares(amount, rows * top, bound, skew, False)
    places = jnp.arange(amount)

    def named(sizes, offset_by):
        used = int((sizes > 0).sum())
        fixed = max(1, used // 4)
        passed = fixed + (places - fixed + offset_by * (used - fixed)) % max(1, amount - fixed)
        return jnp.zeros((amount,), jnp.int32).at[sequence[jnp.where(places < fixed, places, passed)]].set(jnp.asarray(sizes, jnp.int32))

    sizes = jnp.where(number % 4 == 0, named(heavy_load, number // 4), named(common, number - number // 4 - 1))
    mixed = jax.random.permutation(jax.random.fold_in(own, 3), amount)
    source_of, sink = mixed[0:amount // 2 * 2:2], mixed[1:amount // 2 * 2:2]
    margin = jnp.minimum(sizes[source_of] - 1, bound - sizes[sink]) // 2
    margin = jnp.where((source_of == sequence[0]) | (sink == sequence[0]) | (sizes[sink] == 0), 0, jnp.maximum(margin, 0))
    passed = jax.random.randint(jax.random.fold_in(own, 4), (amount // 2,), 0, 1 << 20) % (margin + 1)
    sizes = sizes.at[source_of].add(-passed).at[sink].add(passed)
    members = jnp.searchsorted(jnp.cumsum(sizes), jnp.arange(rows * top), side="right").astype(jnp.int32)
    grid = members.reshape(top, rows).T
    grid = grid[jax.random.permutation(jax.random.fold_in(own, 1), rows)]
    offset_by = jax.random.randint(jax.random.fold_in(own, 2), (rows, 1), 0, top)
    return jnp.take_along_axis(grid, (jnp.arange(top)[None, :] + offset_by) % top, axis=1)


def shares(count, total, reach, lean, full):
    portions = [(1 << 20) // math.isqrt(rank ** lean) + 1 for rank in range(1, count + 1)]
    largest = reach if full else min(reach, max(-(-total // count), total * portions[0] // sum(portions)))
    least = 1 if total - largest >= count - 1 else 0
    holding, spare = [largest] + [least] * (count - 1), total - largest - least * (count - 1)
    while spare > 0:
        movable = [i for i in range(1, count) if holding[i] < largest] or [i for i in range(1, count) if holding[i] < reach]
        whole, remaining = sum([portions[i] for i in movable]), spare
        for i in movable:
            addition = min(reach - holding[i], max(1, remaining * portions[i] // whole), spare)
            holding[i] = holding[i] + addition
            spare = spare - addition
    return np.array(holding)


def normal_values(own_key, extent, scale, limit, cuts=(), kind=jnp.bfloat16):
    drawn = jax.random.normal(own_key, extent, jnp.float32) * scale
    if len(cuts) > 0:
        drawn = level_of(own_key, extent, cuts, -0.22, 0.18) * drawn
    return jnp.clip(drawn, min=-limit, max=limit).astype(kind)


def setup_inputs(seed: int = 0, part: int = 0) -> dict:
    streams_of = jax.random.split(jax.random.key(seed), 12)
    part_splits = jax.random.split(jax.random.fold_in(streams_of[11], part), 12)
    queries = draw_queries(jax.random.fold_in(jax.random.fold_in(streams_of[11], part), 71), part)
    latent_cache = draw_latent_cache(jax.random.fold_in(jax.random.fold_in(streams_of[11], part), 71), part)
    cache_length = draw_cache_length(jax.random.fold_in(jax.random.fold_in(streams_of[11], part), 71), part)
    steal_source = draw_steal_source(jax.random.fold_in(jax.random.fold_in(streams_of[11], part), 71), part)
    hidden = draw_hidden(jax.random.fold_in(jax.random.fold_in(streams_of[11], part), 71), part)
    norm_gain = jnp.clip(1.0 + 0.18 * jax.random.normal(streams_of[5], (D,), jnp.float32), 0.1, 1.9)
    expert_ids_keys = jax.random.split(jax.random.fold_in(part_splits[6], 1), ROWS // REQ)
    expert_ids_turns = jax.random.permutation(jax.random.fold_in(part_splits[6], 3), ROWS // REQ)
    expert_ids = jax.vmap(lambda own, number: assign_block(jax.random.fold_in(part_splits[6], 2), own, number, REQ, EXPERTS, TOP, CAP_E, 2))(expert_ids_keys, expert_ids_turns).reshape((ROWS, TOP))
    expert_weight = jnp.clip(0.05 + 0.39999999 * jax.random.uniform(part_splits[7], (ROWS, TOP), jnp.float32) ** level_of(part_splits[7], (ROWS, TOP), ((0, 16),), -0.2, 0.2), 0.05, 0.45)
    w_gate = normal_values(streams_of[8], (EXPERTS, D, FF), D ** -0.5, 0.0625, ((0, 4), (1, 4)))
    w_up = normal_values(streams_of[9], (EXPERTS, D, FF), D ** -0.5, 0.0625, ((0, 4), (1, 4)))
    w_down = normal_values(streams_of[10], (EXPERTS, FF, D), FF ** -0.5, 0.1875, ((0, 4), (2, 4)))
    return dict(queries=queries, latent_cache=latent_cache, cache_length=cache_length, steal_source=steal_source, hidden=hidden, norm_gain=norm_gain, expert_ids=expert_ids, expert_weight=expert_weight, w_gate=w_gate, w_up=w_up, w_down=w_down)


score_scale = 192.0 ** (-0.5)
norm_eps = 1e-06

def reference(queries, latent_cache, cache_length, steal_source, hidden, norm_gain, expert_ids, expert_weight, w_gate, w_up, w_down):
    rows = queries.shape[0]
    slots = jnp.arange(rows, dtype=jnp.int32)
    column = slots // REQ % N_EP
    anchor = ((steal_source * N_EP + column) * REQ + slots % REQ).astype(jnp.int32)

    def attend_block(block):
        start = (block * REQ).astype(jnp.int32)
        index = lax.dynamic_slice_in_dim(anchor, start, REQ)
        lengths = lax.dynamic_slice_in_dim(cache_length, start, REQ)
        query = queries[index].astype(jnp.float32)
        keys = latent_cache[index].astype(jnp.float32)
        scores = jnp.einsum('rhc,rtc->rht', query, keys) * score_scale
        places = jnp.arange(CAP, dtype=jnp.int32)
        valid = places[None, None, :] < lengths[:, None, None]
        scores = jnp.where(valid, scores, -jnp.inf)
        peak = lax.optimization_barrier(jnp.max(scores, axis=-1, keepdims=True))
        raised = jnp.exp(scores - peak)
        probs = (raised / lax.optimization_barrier(jnp.sum(raised, axis=-1, keepdims=True))).astype(jnp.bfloat16)
        output = jnp.einsum('rht,rtc->rhc', probs.astype(jnp.float32), keys[:, :, :LAT])
        return output.astype(jnp.bfloat16)
    attended = lax.map(attend_block, jnp.arange(rows // REQ, dtype=jnp.int32)).reshape(rows, HEADS, LAT)
    values = hidden.astype(jnp.float32)
    scale = lax.rsqrt(lax.optimization_barrier(jnp.mean(values * values, axis=-1, keepdims=True)) + norm_eps)
    normed = (values * scale * norm_gain).astype(jnp.bfloat16)
    pieces = normed.astype(jnp.float32).reshape(rows, N_STEAL, D // N_STEAL)

    def sliced_sum(weight):
        blocks = weight.astype(jnp.float32).reshape(N_STEAL, D // N_STEAL, FF)
        terms = jnp.einsum('rsk,skf->rsf', pieces, blocks).astype(jnp.bfloat16)
        terms = lax.optimization_barrier(terms)
        return lax.optimization_barrier(jnp.sum(terms.astype(jnp.float32), axis=1))

    def expert_step(total, expert):
        gate = sliced_sum(w_gate[expert])
        up_value = sliced_sum(w_up[expert])
        active = (jax.nn.silu(gate) * up_value).astype(jnp.bfloat16)
        result = jnp.dot(active, w_down[expert], preferred_element_type=jnp.float32).astype(jnp.bfloat16)
        share = lax.optimization_barrier(jnp.sum(jnp.where(expert_ids == expert, expert_weight, jnp.zeros_like(expert_weight)), axis=1))
        return (total + share[:, None] * result.astype(jnp.float32), None)
    total, _ = lax.scan(expert_step, jnp.zeros((rows, D), jnp.float32), jnp.arange(EXPERTS, dtype=jnp.int32))
    return (attended, total.astype(jnp.bfloat16))
```

```python
import jax
import jax.numpy as jnp
from jax import lax
from jax.experimental import pallas as pl
from jax.experimental.pallas import tpu as pltpu
from jax.sharding import PartitionSpec as P

LAT = 512
CAP_E = 12
CHUNKS = 2

score_scale = 192.0 ** (-0.5)
norm_eps = 1e-06

f32, bf16 = jnp.float32, jnp.bfloat16


def xor_permute(x, axis, m):
    size = lax.axis_size(axis)
    return lax.ppermute(x, axis, [(i, i ^ m) for i in range(size)])


def attention_kernel(index_ref, length_ref, q_ref, c_ref, out_ref):
    i = pl.program_id(0)
    cache = c_ref[0]
    scores = lax.dot_general(
        q_ref[0], cache, (((1,), (1,)), ((), ())), preferred_element_type=f32
    )
    scores = scores * score_scale
    places = lax.broadcasted_iota(jnp.int32, scores.shape, 1)
    scores = jnp.where(places < length_ref[i], scores, -jnp.inf)
    peak = jnp.max(scores, axis=-1, keepdims=True)
    raised = jnp.exp(scores - peak)
    probs = (raised / jnp.sum(raised, axis=-1, keepdims=True)).astype(bf16)
    out_ref[0] = jnp.dot(probs, cache[:, :LAT], preferred_element_type=f32).astype(bf16)


def attend(queries, cache, index, lengths, count, slots, first):
    heads, width = queries.shape[1:]
    positions = cache.shape[1]
    return pl.pallas_call(
        attention_kernel,
        grid_spec=pltpu.PrefetchScalarGridSpec(
            num_scalar_prefetch=2,
            grid=(count,),
            in_specs=[
                pl.BlockSpec((1, heads, width), lambda i, idx, n: (idx[i], 0, 0)),
                pl.BlockSpec((1, positions, width), lambda i, idx, n: (idx[i], 0, 0)),
            ],
            out_specs=pl.BlockSpec((1, heads, LAT), lambda i, idx, n: (first + i, 0, 0)),
        ),
        out_shape=jax.ShapeDtypeStruct((slots, heads, LAT), bf16),
        compiler_params=pltpu.CompilerParams(vmem_limit_bytes=8 * 2**20),
        cost_estimate=pl.CostEstimate(
            flops=2 * count * heads * positions * (width + LAT),
            bytes_accessed=count * 2 * (heads * width + positions * width + heads * LAT),
            transcendentals=count * heads * positions,
        ),
    )(index, lengths, queries, cache)


def place_kernel(where_ref, got_ref, all_ref, out_ref):
    del where_ref, all_ref
    out_ref[...] = got_ref[...]


def per_device(
    queries,
    latent_cache,
    cache_length,
    steal_source,
    hidden,
    norm_gain,
    expert_ids,
    expert_weight,
    w_gate,
    w_up,
    w_down,
):
    s, e = lax.axis_index("steal"), lax.axis_index("ep")
    width, experts = lax.axis_size("steal"), lax.axis_size("ep")
    requests, model_width = hidden.shape
    top = expert_ids.shape[1]
    part = model_width // width
    core = s % 2
    lent = width - 1

    values = hidden.astype(f32)
    scale = lax.rsqrt(jnp.mean(values * values, axis=-1, keepdims=True) + norm_eps)
    normed = (values * scale * norm_gain).astype(bf16)

    high = lax.reduce_precision(expert_weight, 8, 7)
    middle = lax.reduce_precision(expert_weight - high, 8, 7)
    low = expert_weight - high - middle
    meta = jnp.concatenate(
        [cache_length.astype(f32)[:, None], expert_ids.astype(f32), high, middle, low], axis=1
    ).astype(bf16)
    meta = jnp.pad(meta, ((0, 0), (0, 128 - meta.shape[1])))

    rows, metas = [], []
    for m in range(width):
        piece = lax.dynamic_slice(normed, (0, (s ^ m) * part), (requests, part))
        if m == 0:
            rows.append(piece)
            metas.append(meta)
        else:
            got = xor_permute(jnp.concatenate([piece, meta], axis=1), "steal", m)
            rows.append(got[:, :part])
            metas.append(got[:, part:])

    slot_ids = jnp.arange(lent, dtype=jnp.int32)
    offset = (s - steal_source[:lent]) % width
    partner = s ^ ((s + offset) % width)
    peer_lengths = jnp.stack([metas[m][:lent, 0] for m in range(1, width)]).astype(jnp.int32)
    is_partner = partner[None, :] == jnp.arange(1, width, dtype=jnp.int32)[:, None]
    order = jnp.sum(jnp.where(is_partner, slot_ids[None, :], 0), axis=1)
    lent_lengths = jnp.sum(jnp.where(is_partner, peer_lengths, 0), axis=1)
    own = requests - lent
    kept = attend(
        queries,
        latent_cache,
        jnp.arange(lent, requests, dtype=jnp.int32),
        cache_length[lent:],
        own,
        requests,
        lent,
    )
    given = attend(queries, latent_cache, order, lent_lengths, lent, lent, 0)
    taken = jnp.stack([xor_permute(given[m - 1], "steal", m) for m in range(1, width)])
    come_from = s ^ steal_source[:lent]
    where = jnp.sum(
        jnp.where(
            come_from[None, :] == jnp.arange(1, width, dtype=jnp.int32)[:, None],
            slot_ids[None, :],
            0,
        ),
        axis=1,
    )
    heads = queries.shape[1]
    attended = pl.pallas_call(
        place_kernel,
        grid_spec=pltpu.PrefetchScalarGridSpec(
            num_scalar_prefetch=1,
            grid=(lent,),
            in_specs=[
                pl.BlockSpec((1, heads, LAT), lambda i, w: (i, 0, 0)),
                pl.BlockSpec(memory_space=pl.ANY),
            ],
            out_specs=pl.BlockSpec((1, heads, LAT), lambda i, w: (w[i], 0, 0)),
        ),
        out_shape=jax.ShapeDtypeStruct(kept.shape, bf16),
        input_output_aliases={2: 0},
        compiler_params=pltpu.CompilerParams(vmem_limit_bytes=4 * 2**20),
    )(where, taken, kept)

    half = w_gate.shape[2] // 2
    gate_send = lax.dynamic_slice(w_gate[0], (0, (1 - core) * half), (part, half))
    gate_keep = lax.dynamic_slice(w_gate[0], (0, core * half), (part, half))
    up_send = lax.dynamic_slice(w_up[0], (0, (1 - core) * half), (part, half))
    up_keep = lax.dynamic_slice(w_up[0], (0, core * half), (part, half))
    down_own = lax.dynamic_slice(w_down[0], (core * half, 0), (half, part))
    down_other = lax.dynamic_slice(w_down[0], ((1 - core) * half, 0), (half, part))
    tokens = jnp.concatenate(rows, axis=0)
    notes = jnp.concatenate(metas, axis=0).astype(f32)
    ids = notes[:, 1 : 1 + top].astype(jnp.int32)
    weights = (
        notes[:, 1 + top : 1 + 2 * top]
        + notes[:, 1 + 2 * top : 1 + 3 * top]
        + notes[:, 1 + 3 * top : 1 + 4 * top]
    )
    targets = e ^ jnp.arange(experts, dtype=jnp.int32)
    named = ids[:, :, None] == targets[None, None, :]
    hit = jnp.any(named, axis=1)
    share = jnp.sum(jnp.where(named, weights[:, :, None], 0.0), axis=1)
    number = jnp.arange(width * requests, dtype=jnp.int32)
    block = number // requests
    ahead = (block[:, None] == block[None, :]) & (number[None, :] < number[:, None])
    rank = jnp.sum((ahead[:, :, None] & hit[None, :, :]).astype(jnp.int32), axis=1)
    piece = CAP_E // CHUNKS
    room = width * piece
    place = (rank // piece) * room + (s ^ block)[:, None] * piece + rank % piece
    spots = jnp.arange(CHUNKS * room, dtype=jnp.int32).reshape(CHUNKS, 1, room, 1)
    select = hit.T[None, :, None, :] & (place.T[None, :, None, :] == spots)
    weight_map = jnp.where(select, share.T[None, :, None, :], 0.0)
    outgoing = jnp.dot(
        select.reshape(CHUNKS * experts * room, width * requests).astype(bf16),
        tokens,
        preferred_element_type=f32,
    ).astype(bf16)
    outgoing = outgoing.reshape(CHUNKS, experts, room, part)

    mixed = jnp.zeros((width * requests, part), f32)
    for chunk in range(CHUNKS):
        arrived = jnp.concatenate(
            [outgoing[chunk, 0]]
            + [xor_permute(outgoing[chunk, n], "ep", n) for n in range(1, experts)],
            axis=0,
        )
        send = jnp.concatenate(
            [
                jnp.dot(arrived, gate_send, preferred_element_type=f32).astype(bf16),
                jnp.dot(arrived, up_send, preferred_element_type=f32).astype(bf16),
            ],
            axis=1,
        )
        got = xor_permute(send, "steal", 1)
        keep = jnp.concatenate(
            [
                jnp.dot(arrived, gate_keep, preferred_element_type=f32),
                jnp.dot(arrived, up_keep, preferred_element_type=f32),
            ],
            axis=1,
        )
        total = (keep + got.astype(f32)).astype(bf16)
        step = 2
        while step < width:
            total = (total.astype(f32) + xor_permute(total, "steal", step).astype(f32)).astype(bf16)
            step *= 2
        total = total.astype(f32)
        active = (jax.nn.silu(total[:, :half]) * total[:, half:]).astype(bf16)
        other = xor_permute(active, "steal", 1)
        produced = (
            jnp.dot(active, down_own, preferred_element_type=f32)
            + jnp.dot(other, down_other, preferred_element_type=f32)
        ).astype(bf16)
        produced = produced.reshape(experts, room, part)
        returned = jnp.concatenate(
            [produced[0]] + [xor_permute(produced[n], "ep", n) for n in range(1, experts)],
            axis=0,
        )
        mixed = mixed + jnp.einsum(
            "ir,ik->rk",
            weight_map[chunk].reshape(experts * room, width * requests),
            returned.astype(f32),
            precision=lax.Precision.HIGHEST,
            preferred_element_type=f32,
        )
    mixed = mixed.astype(bf16).reshape(width, requests, part)
    result = jnp.zeros((requests, model_width), bf16)
    for m in range(width):
        got = mixed[m] if m == 0 else xor_permute(mixed[m], "steal", m)
        result = lax.dynamic_update_slice(result, got, (0, (s ^ m) * part))
    return (attended, result)


def solution(mesh):
    return jax.shard_map(
        per_device,
        mesh=mesh,
        in_specs=(
            P(("rep", "steal", "ep"), None, None),
            P(("rep", "steal", "ep"), None, None),
            P(("rep", "steal", "ep")),
            P(("rep", "steal", "ep")),
            P(("rep", "steal", "ep"), None),
            P(),
            P(("rep", "steal", "ep"), None),
            P(("rep", "steal", "ep"), None),
            P("ep", "steal", None),
            P("ep", "steal", None),
            P("ep", None, "steal"),
        ),
        out_specs=(P(("rep", "steal", "ep"), None, None), P(("rep", "steal", "ep"), None)),
        check_vma=False,
    )
```

```python
import functools

import jax
import jax.numpy as jnp
from jax import lax
from jax.experimental import pallas as pl
from jax.experimental.pallas import tpu as pltpu
from jax.sharding import PartitionSpec as P

LAT = 512
CAP_E = 12
CHUNKS = 2
LANES = 128
ATTEND_VMEM = 12 * 2**20
NOTES = 16

score_scale = 192.0 ** (-0.5)
norm_eps = 1e-06

f32, bf16 = jnp.float32, jnp.bfloat16
vmem = pl.BlockSpec(memory_space=pltpu.VMEM)
hbm = pl.BlockSpec(memory_space=pltpu.HBM)
smem = pl.BlockSpec(memory_space=pltpu.SMEM)


def xor_permute(x, axis, m):
    size = lax.axis_size(axis)
    return lax.ppermute(x, axis, [(i, i ^ m) for i in range(size)])


def prepare_kernel(
    width, here_ref, hidden_ref, gain_ref, length_ref, ids_ref, weight_ref, *refs
):
    messages, (normed_ref, notes_ref) = refs[:width], refs[width:]
    s = here_ref[0]
    requests, model_width = hidden_ref.shape
    part = model_width // width
    top = ids_ref.shape[0]
    values = hidden_ref[...].astype(f32)
    scale = lax.rsqrt(jnp.mean(values * values, axis=-1, keepdims=True) + norm_eps)
    normed_ref[...] = (values * scale * gain_ref[...]).astype(bf16)
    weight = weight_ref[...]
    high = weight.astype(bf16).astype(f32)
    middle = (weight - high).astype(bf16).astype(f32)
    notes_ref[...] = jnp.zeros_like(notes_ref)
    notes_ref[0:1, :] = length_ref[...].astype(f32)
    notes_ref[1 : 1 + top, :] = ids_ref[...].astype(f32)
    notes_ref[1 + top : 1 + 2 * top, :] = high
    notes_ref[1 + 2 * top : 1 + 3 * top, :] = middle
    notes_ref[1 + 3 * top : 1 + 4 * top, :] = weight - high - middle
    source = lax.broadcasted_iota(jnp.int32, (requests, LANES), 0)
    lane = lax.broadcasted_iota(jnp.int32, (requests, LANES), 1)
    blocks = notes_ref.shape[0] // NOTES
    for m in range(width):
        start = pl.multiple_of((s ^ m) * part, LANES)
        messages[m][:, :part] = normed_ref[:, pl.ds(start, part)]
        shift = (lane == source + m * requests).astype(bf16)
        for b in range(blocks):
            notes = notes_ref[b * NOTES : (b + 1) * NOTES, :].astype(bf16)
            messages[m][:, part + b * LANES : part + (b + 1) * LANES] = jnp.dot(
                notes, shift, preferred_element_type=f32
            ).astype(bf16)


def prepare(s, hidden, norm_gain, cache_length, expert_ids, expert_weight, width):
    requests, model_width = hidden.shape
    part = model_width // width
    blocks = -(-(1 + 4 * expert_ids.shape[1]) // NOTES)
    message = jax.ShapeDtypeStruct((requests, part + blocks * LANES), bf16)
    return pl.pallas_call(
        functools.partial(prepare_kernel, width),
        in_specs=[smem] + [vmem] * 5,
        out_specs=[vmem] * width,
        out_shape=[message] * width,
        scratch_shapes=[
            pltpu.VMEM((requests, model_width), bf16),
            pltpu.VMEM((blocks * NOTES, requests), f32),
        ],
        compiler_params=pltpu.CompilerParams(vmem_limit_bytes=56 * 2**20),
        cost_estimate=pl.CostEstimate(
            flops=4 * requests * model_width,
            bytes_accessed=4 * requests * model_width + 4 * model_width,
            transcendentals=requests,
        ),
    )(
        s.reshape(1),
        hidden,
        norm_gain.reshape(1, -1),
        cache_length.reshape(1, -1),
        expert_ids.T,
        expert_weight.T,
    )


def message_groups(experts):
    return [[(chunk, n) for chunk in range(CHUNKS)] for n in range(experts)]


def dispatch_kernel(width, experts, top, requests, here_ref, *refs):
    messages = refs[:width]
    groups = message_groups(experts)
    count = len(groups)
    outs, (map_ref, length_ref) = refs[width : width + count], refs[width + count : width + count + 2]
    tokens_ref, select_ref = refs[width + count + 2 :]
    s, e = here_ref[0], here_ref[1]
    part = tokens_ref.shape[1]
    total = width * requests
    piece = CAP_E // CHUNKS
    room = width * piece
    for m in range(width):
        tokens_ref[m * requests : (m + 1) * requests, :] = messages[m][:, :part]
    blocks = (messages[0].shape[1] - part) // LANES
    notes = []
    for b in range(blocks):
        at = part + b * LANES
        summed = messages[0][:, at : at + LANES].astype(f32)
        for m in range(1, width):
            summed = summed + messages[m][:, at : at + LANES].astype(f32)
        notes.append(summed)
    length_ref[...] = notes[0][0:1, :].astype(jnp.int32)

    def note(k):
        at = k % NOTES
        return notes[k // NOTES][at : at + 1, :total]

    rows = max(8, experts)
    expert = (e ^ lax.broadcasted_iota(jnp.int32, (rows, total), 0)).astype(f32)
    hit = jnp.zeros((rows, total), f32)
    share = jnp.zeros((rows, total), f32)
    for t in range(top):
        same = note(1 + t) == expert
        weight = note(1 + top + t) + note(1 + 2 * top + t) + note(1 + 3 * top + t)
        hit = jnp.where(same, 1.0, hit)
        share = share + jnp.where(same, weight, 0.0)
    shift = requests.bit_length() - 1
    a = lax.broadcasted_iota(jnp.int32, (total, total), 0)
    b = lax.broadcasted_iota(jnp.int32, (total, total), 1)
    ahead = ((lax.shift_right_logical(a, shift) == lax.shift_right_logical(b, shift)) & (a < b)).astype(bf16)
    rank = jnp.dot(hit.astype(bf16), ahead, preferred_element_type=f32).astype(jnp.int32)
    lane = lax.broadcasted_iota(jnp.int32, (1, total), 1)
    base = (s ^ lax.shift_right_logical(lane, shift)) * piece
    spot = lax.broadcasted_iota(jnp.int32, (room, total), 0)
    for chunk in range(CHUNKS):
        for n in range(experts):
            local = rank[n : n + 1, :] - chunk * piece
            inside = (hit[n : n + 1, :] > 0.5) & (local >= 0) & (local < piece)
            chosen = jnp.where(inside, base + local, -1) == spot
            at = (chunk * experts + n) * room
            select_ref[at : at + room, :] = jnp.where(chosen, 1.0, 0.0)
            map_ref[at : at + room, :] = jnp.where(chosen, share[n : n + 1, :], 0.0)
    select = select_ref[...].astype(bf16)
    tile = 256 if part % 256 == 0 else LANES
    for at in range(0, part, tile):
        sent = jnp.dot(select, tokens_ref[:, at : at + tile], preferred_element_type=f32)
        for out, group in zip(outs, groups):
            pieces = [
                sent[(chunk * experts + n) * room : (chunk * experts + n + 1) * room, :]
                for chunk, n in group
            ]
            out[:, at : at + tile] = jnp.concatenate(pieces, axis=0).astype(bf16)


def dispatch(s, e, messages, part, experts, top):
    width = len(messages)
    requests = messages[0].shape[0]
    room = width * CAP_E // CHUNKS
    groups = message_groups(experts)
    places = CHUNKS * experts * room
    total = width * requests
    *outs, weight_map, lengths = pl.pallas_call(
        functools.partial(dispatch_kernel, width, experts, top, requests),
        in_specs=[smem] + [vmem] * width,
        out_specs=[vmem] * (len(groups) + 2),
        out_shape=[jax.ShapeDtypeStruct((len(group) * room, part), bf16) for group in groups]
        + [
            jax.ShapeDtypeStruct((places, total), f32),
            jax.ShapeDtypeStruct((1, LANES), jnp.int32),
        ],
        scratch_shapes=[
            pltpu.VMEM((total, part), bf16),
            pltpu.VMEM((places, total), f32),
        ],
        compiler_params=pltpu.CompilerParams(vmem_limit_bytes=16 * 2**20),
        cost_estimate=pl.CostEstimate(
            flops=2 * places * total * part,
            bytes_accessed=2 * part * (total + places),
            transcendentals=0,
        ),
    )(jnp.stack([s, e]).astype(jnp.int32), *messages)
    return outs, weight_map, lengths


def attend_all(queries, caches, lengths):
    scores = [
        lax.dot_general(cache, query, (((0,), (0,)), ((), ())), preferred_element_type=f32)
        for query, cache in zip(queries, caches)
    ]
    probs = []
    for score, length in zip(scores, lengths):
        score = score * score_scale
        places = lax.broadcasted_iota(jnp.int32, score.shape, 0)
        score = jnp.where(places < length, score, -jnp.inf)
        raised = jnp.exp(score - jnp.max(score, axis=0, keepdims=True))
        share = raised * (1.0 / jnp.sum(raised, axis=0, keepdims=True))
        probs.append(share.astype(bf16).T)
    return [
        lax.dot_general(
            prob, cache[:LAT], (((1,), (1,)), ((), ())), preferred_element_type=f32
        ).astype(bf16)
        for prob, cache in zip(probs, caches)
    ]


def attend_cost(count, heads, positions, width):
    return pl.CostEstimate(
        flops=2 * count * heads * positions * (width + LAT),
        bytes_accessed=count * 2 * (heads * width + positions * width + heads * LAT),
        transcendentals=count * heads * positions,
    )


def kept_kernel(step, length_ref, q_ref, c_ref, out_ref):
    i = pl.program_id(0)
    outs = attend_all(
        [q_ref[j] for j in range(step)],
        [c_ref[j] for j in range(step)],
        [length_ref[i * step + j] for j in range(step)],
    )
    for j in range(step):
        out_ref[j] = outs[j]


def attend_kept(queries, cache, lengths):
    count, width, heads = queries.shape
    positions = cache.shape[2]
    step = next(k for k in (8, 4, 2, 1) if count % k == 0)
    return pl.pallas_call(
        functools.partial(kept_kernel, step),
        grid_spec=pltpu.PrefetchScalarGridSpec(
            num_scalar_prefetch=1,
            grid=(count // step,),
            in_specs=[
                pl.BlockSpec((step, width, heads), lambda i, n: (i, 0, 0)),
                pl.BlockSpec((step, width, positions), lambda i, n: (i, 0, 0)),
            ],
            out_specs=pl.BlockSpec((step, heads, LAT), lambda i, n: (i, 0, 0)),
        ),
        out_shape=jax.ShapeDtypeStruct((count, heads, LAT), bf16),
        compiler_params=pltpu.CompilerParams(vmem_limit_bytes=ATTEND_VMEM),
        cost_estimate=attend_cost(count, heads, positions, width),
    )(lengths, queries, cache)


def lent_kernel(lent, index_ref, length_ref, *refs):
    outs = attend_all(
        [refs[i][0] for i in range(lent)],
        [refs[lent + i][0] for i in range(lent)],
        [length_ref[i] for i in range(lent)],
    )
    for i in range(lent):
        refs[2 * lent + i][...] = outs[i]


def attend_lent(queries, cache, index, lengths):
    lent = index.shape[0]
    _, width, heads = queries.shape
    positions = cache.shape[2]

    def at(i):
        return lambda step, idx, n: (idx[i], 0, 0)

    return pl.pallas_call(
        functools.partial(lent_kernel, lent),
        grid_spec=pltpu.PrefetchScalarGridSpec(
            num_scalar_prefetch=2,
            grid=(1,),
            in_specs=[pl.BlockSpec((1, width, heads), at(i)) for i in range(lent)]
            + [pl.BlockSpec((1, width, positions), at(i)) for i in range(lent)],
            out_specs=[pl.BlockSpec((heads, LAT), lambda step, idx, n: (0, 0))] * lent,
        ),
        out_shape=[jax.ShapeDtypeStruct((heads, LAT), bf16)] * lent,
        compiler_params=pltpu.CompilerParams(vmem_limit_bytes=ATTEND_VMEM),
        cost_estimate=attend_cost(lent, heads, positions, width),
    )(index, lengths, *[queries] * lent, *[cache] * lent)


def place_kernel(lent, where_ref, *refs):
    out_ref, sems = refs[lent + 1], refs[lent + 2]
    copies = [
        pltpu.make_async_copy(refs[i], out_ref.at[where_ref[i]], sems.at[i]) for i in range(lent)
    ]
    for copy in copies:
        copy.start()
    for copy in copies:
        copy.wait()


def place(where, taken, kept):
    lent = len(taken)
    return pl.pallas_call(
        functools.partial(place_kernel, lent),
        in_specs=[smem] + [pl.BlockSpec(memory_space=pl.ANY)] * lent + [hbm],
        out_specs=hbm,
        out_shape=jax.ShapeDtypeStruct(kept.shape, kept.dtype),
        scratch_shapes=[pltpu.SemaphoreType.DMA((lent,))],
        input_output_aliases={lent + 1: 0},
        compiler_params=pltpu.CompilerParams(vmem_limit_bytes=2 * 2**20),
    )(where, *taken, kept)


def total_sum(total, width):
    step = 2
    while step < width:
        total = (total.astype(f32) + xor_permute(total, "steal", step).astype(f32)).astype(bf16)
        step *= 2
    return total


def per_device(
    queries,
    latent_cache,
    cache_length,
    steal_source,
    hidden,
    norm_gain,
    expert_ids,
    expert_weight,
    w_gate,
    w_up,
    w_down,
):
    s, e = lax.axis_index("steal"), lax.axis_index("ep")
    width, experts = lax.axis_size("steal"), lax.axis_size("ep")
    requests, model_width = hidden.shape
    top = expert_ids.shape[1]
    part = model_width // width
    core = s % 2
    lent = width - 1

    messages = prepare(s, hidden, norm_gain, cache_length, expert_ids, expert_weight, width)
    messages = [messages[0]] + [xor_permute(messages[m], "steal", m) for m in range(1, width)]
    outgoing, weight_map, peer_lengths = dispatch(s, e, messages, part, experts, top)
    outgoing, peer_lengths = lax.optimization_barrier((outgoing, peer_lengths))
    room = width * CAP_E // CHUNKS
    pieces = {}
    for sent, group in zip(outgoing, message_groups(experts)):
        n = group[0][1]
        got = sent if n == 0 else xor_permute(sent, "ep", n)
        for at, key in enumerate(group):
            pieces[key] = got[at * room : (at + 1) * room]

    slot_ids = jnp.arange(lent, dtype=jnp.int32)
    others = jnp.arange(1, width, dtype=jnp.int32)[:, None]
    peer_lengths = peer_lengths[0, : width * requests].reshape(width, requests)[1:, :lent]
    partner = s ^ ((2 * s - steal_source[:lent]) % width)
    is_partner = partner[None, :] == others
    order = jnp.sum(jnp.where(is_partner, slot_ids[None, :], 0), axis=1)
    lent_lengths = jnp.sum(jnp.where(is_partner, peer_lengths, 0), axis=1)
    comes_from = (s ^ steal_source[:lent])[None, :] == others
    where = jnp.sum(jnp.where(comes_from, slot_ids[None, :], 0), axis=1)
    queries, cache = queries.swapaxes(1, 2), latent_cache.swapaxes(1, 2)
    given = attend_lent(queries, cache, order, lent_lengths)
    lengths, given = lax.optimization_barrier((cache_length, given))
    taken = [xor_permute(given[m - 1], "steal", m) for m in range(1, width)]
    kept = attend_kept(queries, cache, lengths)
    pieces, kept = lax.optimization_barrier((pieces, kept))

    half = w_gate.shape[2] // 2
    gate_send = lax.dynamic_slice(w_gate[0], (0, (1 - core) * half), (part, half))
    gate_keep = lax.dynamic_slice(w_gate[0], (0, core * half), (part, half))
    up_send = lax.dynamic_slice(w_up[0], (0, (1 - core) * half), (part, half))
    up_keep = lax.dynamic_slice(w_up[0], (0, core * half), (part, half))
    down_own = lax.dynamic_slice(w_down[0], (core * half, 0), (half, part))
    down_other = lax.dynamic_slice(w_down[0], ((1 - core) * half, 0), (half, part))

    mixed = jnp.zeros((width * requests, part), f32)
    for chunk in range(CHUNKS):
        arrived = [pieces[chunk, n] for n in range(experts)]
        arrived = jnp.concatenate(arrived, axis=0)
        send = jnp.concatenate(
            [
                jnp.dot(arrived, gate_send, preferred_element_type=f32).astype(bf16),
                jnp.dot(arrived, up_send, preferred_element_type=f32).astype(bf16),
            ],
            axis=1,
        )
        got = xor_permute(send, "steal", 1)
        keep = jnp.concatenate(
            [
                jnp.dot(arrived, gate_keep, preferred_element_type=f32),
                jnp.dot(arrived, up_keep, preferred_element_type=f32),
            ],
            axis=1,
        )
        total = (keep + got.astype(f32)).astype(bf16)
        if chunk == 0:
            total, taken = lax.optimization_barrier((total, taken))
        total = total_sum(total, width)
        if chunk == 0:
            attended = place(where, taken, kept)
            total, attended = lax.optimization_barrier((total, attended))
        total = total.astype(f32)
        active = (jax.nn.silu(total[:, :half]) * total[:, half:]).astype(bf16)
        other = xor_permute(active, "steal", 1)
        produced = (
            jnp.dot(active, down_own, preferred_element_type=f32)
            + jnp.dot(other, down_other, preferred_element_type=f32)
        ).astype(bf16)
        produced = produced.reshape(experts, room, part)
        returned = jnp.concatenate(
            [produced[0]] + [xor_permute(produced[n], "ep", n) for n in range(1, experts)],
            axis=0,
        )
        mixed = mixed + jnp.einsum(
            "ir,ik->rk",
            weight_map[chunk * experts * room : (chunk + 1) * experts * room],
            returned.astype(f32),
            precision=lax.Precision.HIGHEST,
            preferred_element_type=f32,
        )
    mixed = mixed.astype(bf16).reshape(width, requests, part)
    result = jnp.zeros((requests, model_width), bf16)
    for m in range(width):
        got = mixed[m] if m == 0 else xor_permute(mixed[m], "steal", m)
        result = lax.dynamic_update_slice(result, got, (0, (s ^ m) * part))
    return (attended, result)


def solution(mesh):
    return jax.shard_map(
        per_device,
        mesh=mesh,
        in_specs=(
            P(("rep", "steal", "ep"), None, None),
            P(("rep", "steal", "ep"), None, None),
            P(("rep", "steal", "ep")),
            P(("rep", "steal", "ep")),
            P(("rep", "steal", "ep"), None),
            P(),
            P(("rep", "steal", "ep"), None),
            P(("rep", "steal", "ep"), None),
            P("ep", "steal", None),
            P("ep", "steal", None),
            P("ep", None, "steal"),
        ),
        out_specs=(P(("rep", "steal", "ep"), None, None), P(("rep", "steal", "ep"), None)),
        check_vma=False,
    )
```

```python
import functools

import jax
import jax.numpy as jnp
from jax import lax
from jax.experimental import pallas as pl
from jax.experimental.pallas import tpu as pltpu
from jax.sharding import PartitionSpec as P

LAT = 512
CAP_E = 12
CORES = 2
LANES = 128
ATTEND_VMEM = 12 * 2**20
NOTES = 16

score_scale = 192.0 ** (-0.5)
norm_eps = 1e-06

f32, bf16 = jnp.float32, jnp.bfloat16
vmem = pl.BlockSpec(memory_space=pltpu.VMEM)
hbm = pl.BlockSpec(memory_space=pltpu.HBM)
smem = pl.BlockSpec(memory_space=pltpu.SMEM)

little = pl.CostEstimate(flops=0, bytes_accessed=0, transcendentals=0)


def xor_permute(x, axis, m):
    size = lax.axis_size(axis)
    return lax.ppermute(x, axis, [(i, i ^ m) for i in range(size)])


def prepare_kernel(
    width, here_ref, hidden_ref, gain_ref, length_ref, ids_ref, weight_ref, *refs
):
    messages, (normed_ref, notes_ref) = refs[:width], refs[width:]
    s = here_ref[0]
    requests, model_width = hidden_ref.shape
    part = model_width // width
    top = ids_ref.shape[0]
    values = hidden_ref[...].astype(f32)
    scale = lax.rsqrt(jnp.mean(values * values, axis=-1, keepdims=True) + norm_eps)
    normed_ref[...] = (values * scale * gain_ref[...]).astype(bf16)
    weight = weight_ref[...]
    high = weight.astype(bf16).astype(f32)
    middle = (weight - high).astype(bf16).astype(f32)
    notes_ref[...] = jnp.zeros_like(notes_ref)
    notes_ref[0:1, :] = length_ref[...].astype(f32)
    notes_ref[1 : 1 + top, :] = ids_ref[...].astype(f32)
    notes_ref[1 + top : 1 + 2 * top, :] = high
    notes_ref[1 + 2 * top : 1 + 3 * top, :] = middle
    notes_ref[1 + 3 * top : 1 + 4 * top, :] = weight - high - middle
    source = lax.broadcasted_iota(jnp.int32, (requests, LANES), 0)
    lane = lax.broadcasted_iota(jnp.int32, (requests, LANES), 1)
    blocks = notes_ref.shape[0] // NOTES
    for m in range(width):
        start = pl.multiple_of((s ^ m) * part, LANES)
        messages[m][:, :part] = normed_ref[:, pl.ds(start, part)]
        shift = (lane == source + m * requests).astype(bf16)
        for b in range(blocks):
            notes = notes_ref[b * NOTES : (b + 1) * NOTES, :].astype(bf16)
            messages[m][:, part + b * LANES : part + (b + 1) * LANES] = jnp.dot(
                notes, shift, preferred_element_type=f32
            ).astype(bf16)


def prepare(s, hidden, norm_gain, cache_length, expert_ids, expert_weight, width):
    requests, model_width = hidden.shape
    part = model_width // width
    blocks = -(-(1 + 4 * expert_ids.shape[1]) // NOTES)
    message = jax.ShapeDtypeStruct((requests, part + blocks * LANES), bf16)
    return pl.pallas_call(
        functools.partial(prepare_kernel, width),
        in_specs=[smem] + [vmem] * 5,
        out_specs=[vmem] * width,
        out_shape=[message] * width,
        scratch_shapes=[
            pltpu.VMEM((requests, model_width), bf16),
            pltpu.VMEM((blocks * NOTES, requests), f32),
        ],
        compiler_params=pltpu.CompilerParams(vmem_limit_bytes=56 * 2**20),
        cost_estimate=little,
    )(
        s.reshape(1),
        hidden,
        norm_gain.reshape(1, -1),
        cache_length.reshape(1, -1),
        expert_ids.T,
        expert_weight.T,
    )


def dispatch_kernel(senders, experts, top, requests, here_ref, *refs):
    messages, refs = refs[:senders], refs[senders:]
    outs, (map_ref, length_ref, tokens_ref, select_ref) = refs[:experts], refs[experts:]
    s, e = here_ref[0], here_ref[1]
    part = tokens_ref.shape[1]
    total = senders * requests
    room = senders * CAP_E
    for i in range(senders):
        tokens_ref[i * requests : (i + 1) * requests, :] = messages[i][:, :part]
    notes = []
    for at in range(part, messages[0].shape[1], LANES):
        summed = messages[0][:, at : at + LANES].astype(f32)
        for i in range(1, senders):
            summed = summed + messages[i][:, at : at + LANES].astype(f32)
        notes.append(summed)
    length_ref[...] = notes[0][0:1, :].astype(jnp.int32)

    def note(k):
        at = k % NOTES
        return notes[k // NOTES][at : at + 1, :total]

    rows = max(8, experts)
    expert = (e ^ lax.broadcasted_iota(jnp.int32, (rows, total), 0)).astype(f32)
    hit = jnp.zeros((rows, total), f32)
    share = jnp.zeros((rows, total), f32)
    for t in range(top):
        same = note(1 + t) == expert
        weight = note(1 + top + t) + note(1 + 2 * top + t) + note(1 + 3 * top + t)
        hit = jnp.where(same, 1.0, hit)
        share = share + jnp.where(same, weight, 0.0)
    shift = requests.bit_length() - 1
    a = lax.broadcasted_iota(jnp.int32, (total, total), 0)
    b = lax.broadcasted_iota(jnp.int32, (total, total), 1)
    same_sender = lax.shift_right_logical(a, shift) == lax.shift_right_logical(b, shift)
    ahead = (same_sender & (a < b)).astype(bf16)
    rank = jnp.dot(hit.astype(bf16), ahead, preferred_element_type=f32).astype(jnp.int32)
    lane = lax.broadcasted_iota(jnp.int32, (1, total), 1)
    base = (lax.shift_right_logical(lane, shift) ^ (s & 1)) * CAP_E
    spot = lax.broadcasted_iota(jnp.int32, (room, total), 0)
    for n in range(experts):
        inside = (hit[n : n + 1, :] > 0.5) & (rank[n : n + 1, :] < CAP_E)
        chosen = jnp.where(inside, base + rank[n : n + 1, :], -1) == spot
        select_ref[n * room : (n + 1) * room, :] = jnp.where(chosen, 1.0, 0.0)
        map_ref[n * room : (n + 1) * room, :] = jnp.where(chosen, share[n : n + 1, :], 0.0)
    select = select_ref[...].astype(bf16)
    tile = 256 if part % 256 == 0 else LANES
    for at in range(0, part, tile):
        sent = jnp.dot(select, tokens_ref[:, at : at + tile], preferred_element_type=f32)
        for n in range(experts):
            outs[n][:, at : at + tile] = sent[n * room : (n + 1) * room, :].astype(bf16)


def dispatch(s, e, messages, part, experts, top):
    senders = len(messages)
    requests = messages[0].shape[0]
    room, total = senders * CAP_E, senders * requests
    *outs, weight_map, lengths = pl.pallas_call(
        functools.partial(dispatch_kernel, senders, experts, top, requests),
        in_specs=[smem] + [vmem] * senders,
        out_specs=[vmem] * (experts + 2),
        out_shape=[jax.ShapeDtypeStruct((room, part), bf16)] * experts
        + [
            jax.ShapeDtypeStruct((experts * room, total), f32),
            jax.ShapeDtypeStruct((1, LANES), jnp.int32),
        ],
        scratch_shapes=[
            pltpu.VMEM((total, part), bf16),
            pltpu.VMEM((experts * room, total), f32),
        ],
        compiler_params=pltpu.CompilerParams(vmem_limit_bytes=16 * 2**20),
        cost_estimate=little,
    )(jnp.stack([s, e]).astype(jnp.int32), *messages)
    return outs, weight_map, lengths[0, :total].reshape(senders, requests)


def attend_all(queries, caches, lengths):
    scores = [
        lax.dot_general(cache, query, (((0,), (0,)), ((), ())), preferred_element_type=f32)
        for query, cache in zip(queries, caches)
    ]
    probs = []
    for score, length in zip(scores, lengths):
        score = score * score_scale
        places = lax.broadcasted_iota(jnp.int32, score.shape, 0)
        score = jnp.where(places < length, score, -jnp.inf)
        raised = jnp.exp(score - jnp.max(score, axis=0, keepdims=True))
        share = raised * (1.0 / jnp.sum(raised, axis=0, keepdims=True))
        probs.append(share.astype(bf16).T)
    return [
        lax.dot_general(
            prob, cache[:LAT], (((1,), (1,)), ((), ())), preferred_element_type=f32
        ).astype(bf16)
        for prob, cache in zip(probs, caches)
    ]


def attend_cost(count, heads, positions, width):
    return pl.CostEstimate(
        flops=2 * count * heads * positions * (width + LAT),
        bytes_accessed=count * 2 * (heads * width + positions * width + heads * LAT),
        transcendentals=count * heads * positions,
    )


def kept_kernel(step, length_ref, q_ref, c_ref, out_ref):
    i = pl.program_id(0)
    outs = attend_all(
        [q_ref[j] for j in range(step)],
        [c_ref[j] for j in range(step)],
        [length_ref[i * step + j] for j in range(step)],
    )
    for j in range(step):
        out_ref[j] = outs[j]


def attend_kept(queries, cache, lengths):
    count, width, heads = queries.shape
    positions = cache.shape[2]
    step = next(k for k in (8, 4, 2, 1) if count % k == 0)
    return pl.pallas_call(
        functools.partial(kept_kernel, step),
        grid_spec=pltpu.PrefetchScalarGridSpec(
            num_scalar_prefetch=1,
            grid=(count // step,),
            in_specs=[
                pl.BlockSpec((step, width, heads), lambda i, n: (i, 0, 0)),
                pl.BlockSpec((step, width, positions), lambda i, n: (i, 0, 0)),
            ],
            out_specs=pl.BlockSpec((step, heads, LAT), lambda i, n: (i, 0, 0)),
        ),
        out_shape=jax.ShapeDtypeStruct((count, heads, LAT), bf16),
        compiler_params=pltpu.CompilerParams(vmem_limit_bytes=ATTEND_VMEM),
        cost_estimate=attend_cost(count, heads, positions, width),
    )(lengths, queries, cache)


def lent_kernel(lent, index_ref, length_ref, *refs):
    outs = attend_all(
        [refs[i][0] for i in range(lent)],
        [refs[lent + i][0] for i in range(lent)],
        [length_ref[i] for i in range(lent)],
    )
    for i in range(lent):
        refs[2 * lent + i][...] = outs[i]


def attend_lent(queries, cache, index, lengths):
    lent = index.shape[0]
    _, width, heads = queries.shape
    positions = cache.shape[2]

    def at(i):
        return lambda step, idx, n: (idx[i], 0, 0)

    return pl.pallas_call(
        functools.partial(lent_kernel, lent),
        grid_spec=pltpu.PrefetchScalarGridSpec(
            num_scalar_prefetch=2,
            grid=(1,),
            in_specs=[pl.BlockSpec((1, width, heads), at(i)) for i in range(lent)]
            + [pl.BlockSpec((1, width, positions), at(i)) for i in range(lent)],
            out_specs=[pl.BlockSpec((heads, LAT), lambda step, idx, n: (0, 0))] * lent,
        ),
        out_shape=[jax.ShapeDtypeStruct((heads, LAT), bf16)] * lent,
        compiler_params=pltpu.CompilerParams(vmem_limit_bytes=ATTEND_VMEM),
        cost_estimate=attend_cost(lent, heads, positions, width),
    )(index, lengths, *[queries] * lent, *[cache] * lent)


def place_kernel(lent, where_ref, *refs):
    out_ref, sems = refs[lent + 1], refs[lent + 2]
    copies = [
        pltpu.make_async_copy(refs[i], out_ref.at[where_ref[i]], sems.at[i]) for i in range(lent)
    ]
    for copy in copies:
        copy.start()
    for copy in copies:
        copy.wait()


def place(where, taken, kept):
    lent = len(taken)
    return pl.pallas_call(
        functools.partial(place_kernel, lent),
        in_specs=[smem] + [pl.BlockSpec(memory_space=pl.ANY)] * lent + [hbm],
        out_specs=hbm,
        out_shape=jax.ShapeDtypeStruct(kept.shape, kept.dtype),
        scratch_shapes=[pltpu.SemaphoreType.DMA((lent,))],
        input_output_aliases={lent + 1: 0},
        compiler_params=pltpu.CompilerParams(vmem_limit_bytes=2 * 2**20),
    )(where, *taken, kept)


def total_sum(total, width, first):
    step = 2
    while step < width:
        got = xor_permute(total, "steal", step)
        if first is not None:
            got, first = lax.optimization_barrier((got, first))
        total = (total.astype(f32) + got.astype(f32)).astype(bf16)
        step *= 2
    return total, first


def per_device(
    queries,
    latent_cache,
    cache_length,
    steal_source,
    hidden,
    norm_gain,
    expert_ids,
    expert_weight,
    w_gate,
    w_up,
    w_down,
):
    s, e = lax.axis_index("steal"), lax.axis_index("ep")
    width, experts = lax.axis_size("steal"), lax.axis_size("ep")
    requests, model_width = hidden.shape
    top = expert_ids.shape[1]
    part = model_width // width
    core = s % 2
    lent = width - 1

    messages = prepare(s, hidden, norm_gain, cache_length, expert_ids, expert_weight, width)
    messages = [messages[0]] + [xor_permute(messages[m], "steal", m) for m in range(1, width)]
    outgoing, weight_map, peer_lengths = dispatch(s, e, messages, part, experts, top)
    outgoing, peer_lengths = lax.optimization_barrier((outgoing, peer_lengths))
    pieces = [outgoing[0]] + [xor_permute(outgoing[n], "ep", n) for n in range(1, experts)]

    slot_ids = jnp.arange(lent, dtype=jnp.int32)
    others = jnp.arange(1, width, dtype=jnp.int32)[:, None]
    peer_lengths = peer_lengths[1:, :lent]
    partner = s ^ ((2 * s - steal_source[:lent]) % width)
    is_partner = partner[None, :] == others
    order = jnp.sum(jnp.where(is_partner, slot_ids[None, :], 0), axis=1)
    lent_lengths = jnp.sum(jnp.where(is_partner, peer_lengths, 0), axis=1)
    comes_from = (s ^ steal_source[:lent])[None, :] == others
    where = jnp.sum(jnp.where(comes_from, slot_ids[None, :], 0), axis=1)
    queries, cache = queries.swapaxes(1, 2), latent_cache.swapaxes(1, 2)
    given = attend_lent(queries, cache, order, lent_lengths)
    lengths, given = lax.optimization_barrier((cache_length, given))
    taken = [xor_permute(given[m - 1], "steal", m) for m in range(1, width)]
    kept = attend_kept(queries, cache, lengths)
    pieces, kept = lax.optimization_barrier((pieces, kept))

    half = w_gate.shape[2] // 2
    gate_send = lax.dynamic_slice(w_gate[0], (0, (1 - core) * half), (part, half))
    gate_keep = lax.dynamic_slice(w_gate[0], (0, core * half), (part, half))
    up_send = lax.dynamic_slice(w_up[0], (0, (1 - core) * half), (part, half))
    up_keep = lax.dynamic_slice(w_up[0], (0, core * half), (part, half))
    down_own = lax.dynamic_slice(w_down[0], (core * half, 0), (half, part))
    down_other = lax.dynamic_slice(w_down[0], ((1 - core) * half, 0), (half, part))

    chips, chip = width // CORES, s // CORES
    room = CORES * CAP_E
    arrived = [
        jnp.concatenate([pieces[n][j * room : (j + 1) * room] for n in range(experts)], axis=0)
        for j in range(chips)
    ]
    by_distance = jnp.stack(arrived)
    results = []
    total_before, produced_before = None, None
    for chunk in range(chips):
        arrived = lax.dynamic_index_in_dim(by_distance, chip ^ chunk, 0, keepdims=False)
        if chunk > 0:
            arrived, total_before = lax.optimization_barrier((arrived, total_before))
        send = jnp.concatenate(
            [
                jnp.dot(arrived, gate_send, preferred_element_type=f32).astype(bf16),
                jnp.dot(arrived, up_send, preferred_element_type=f32).astype(bf16),
            ],
            axis=1,
        )
        got = xor_permute(send, "steal", 1)
        keep = jnp.concatenate(
            [
                jnp.dot(arrived, gate_keep, preferred_element_type=f32),
                jnp.dot(arrived, up_keep, preferred_element_type=f32),
            ],
            axis=1,
        )
        total = (keep + got.astype(f32)).astype(bf16)
        if chunk == 0:
            total, taken = lax.optimization_barrier((total, taken))
        total_before = total
        total, produced_before = total_sum(total, width, produced_before)
        if chunk == 0:
            attended = place(where, taken, kept)
            total, attended = lax.optimization_barrier((total, attended))
        total = total.astype(f32)
        active = (jax.nn.silu(total[:, :half]) * total[:, half:]).astype(bf16)
        other = xor_permute(active, "steal", 1)
        produced = (
            jnp.dot(active, down_own, preferred_element_type=f32)
            + jnp.dot(other, down_other, preferred_element_type=f32)
        ).astype(bf16)
        produced_before = produced
        results.append(produced.reshape(experts, room, part))

    results = jnp.stack(results)
    back = [lax.dynamic_index_in_dim(results, chip ^ j, 0, keepdims=False) for j in range(chips)]
    far = jnp.concatenate(back[1:], axis=1)
    near = back[0]
    far_rows = far.shape[1]
    both = xor_permute(jnp.concatenate([far[1], near[1]], axis=0), "ep", 1)
    far = [far[0], both[:far_rows]] + [xor_permute(far[n], "ep", n) for n in range(2, experts)]
    near = [near[0], both[far_rows:]] + [xor_permute(near[n], "ep", n) for n in range(2, experts)]

    def mix(weight_map, returned):
        returned = jnp.concatenate(returned, axis=0).astype(f32)
        mixed = jnp.einsum(
            "ir,ik->rk",
            weight_map,
            returned,
            precision=lax.Precision.HIGHEST,
            preferred_element_type=f32,
        )
        return mixed.astype(bf16).reshape(-1, requests, part)

    weight_map = weight_map.reshape(experts, width * CAP_E, width * requests)
    split = CORES * requests
    mixed = mix(weight_map[:, room:, split:].reshape(-1, width * requests - split), far)
    got = [xor_permute(mixed[m - CORES], "steal", m) for m in range(CORES, width)]
    near, got = lax.optimization_barrier((near, got))
    mixed = mix(weight_map[:, :room, :split].reshape(-1, split), near)
    got = [mixed[0], xor_permute(mixed[1], "steal", 1)] + got
    result = jnp.zeros((requests, model_width), bf16)
    for m in range(width):
        result = lax.dynamic_update_slice(result, got[m], (0, (s ^ m) * part))
    return (attended, result)


def solution(mesh):
    return jax.shard_map(
        per_device,
        mesh=mesh,
        in_specs=(
            P(("rep", "steal", "ep"), None, None),
            P(("rep", "steal", "ep"), None, None),
            P(("rep", "steal", "ep")),
            P(("rep", "steal", "ep")),
            P(("rep", "steal", "ep"), None),
            P(),
            P(("rep", "steal", "ep"), None),
            P(("rep", "steal", "ep"), None),
            P("ep", "steal", None),
            P("ep", "steal", None),
            P("ep", None, "steal"),
        ),
        out_specs=(P(("rep", "steal", "ep"), None, None), P(("rep", "steal", "ep"), None)),
        check_vma=False,
    )
```

```python
import functools

import jax
import jax.numpy as jnp
from jax import lax
from jax.experimental import pallas as pl
from jax.experimental.pallas import tpu as pltpu
from jax.sharding import PartitionSpec as P

LAT = 512
CAP_E = 12
CORES = 2
LANES = 128
ATTEND_VMEM = 12 * 2**20
NOTES = 16

score_scale = 192.0 ** (-0.5)
norm_eps = 1e-06

f32, bf16 = jnp.float32, jnp.bfloat16
vmem = pl.BlockSpec(memory_space=pltpu.VMEM)
hbm = pl.BlockSpec(memory_space=pltpu.HBM)
smem = pl.BlockSpec(memory_space=pltpu.SMEM)

little = pl.CostEstimate(flops=0, bytes_accessed=0, transcendentals=0)


def xor_permute(x, axis, m):
    size = lax.axis_size(axis)
    return lax.ppermute(x, axis, [(i, i ^ m) for i in range(size)])


def prepare_kernel(
    width, here_ref, hidden_ref, gain_ref, length_ref, ids_ref, weight_ref, *refs
):
    messages, (normed_ref, notes_ref) = refs[:width], refs[width:]
    s = here_ref[0]
    requests, model_width = hidden_ref.shape
    part = model_width // width
    top = ids_ref.shape[0]
    values = hidden_ref[...].astype(f32)
    scale = lax.rsqrt(jnp.mean(values * values, axis=-1, keepdims=True) + norm_eps)
    normed_ref[...] = (values * scale * gain_ref[...]).astype(bf16)
    weight = weight_ref[...]
    high = weight.astype(bf16).astype(f32)
    middle = (weight - high).astype(bf16).astype(f32)
    notes_ref[...] = jnp.zeros_like(notes_ref)
    notes_ref[0:1, :] = length_ref[...].astype(f32)
    notes_ref[1 : 1 + top, :] = ids_ref[...].astype(f32)
    notes_ref[1 + top : 1 + 2 * top, :] = high
    notes_ref[1 + 2 * top : 1 + 3 * top, :] = middle
    notes_ref[1 + 3 * top : 1 + 4 * top, :] = weight - high - middle
    source = lax.broadcasted_iota(jnp.int32, (requests, LANES), 0)
    lane = lax.broadcasted_iota(jnp.int32, (requests, LANES), 1)
    blocks = notes_ref.shape[0] // NOTES
    for m in range(width):
        start = pl.multiple_of((s ^ m) * part, LANES)
        messages[m][:, :part] = normed_ref[:, pl.ds(start, part)]
        shift = (lane == source + m * requests).astype(bf16)
        for b in range(blocks):
            notes = notes_ref[b * NOTES : (b + 1) * NOTES, :].astype(bf16)
            messages[m][:, part + b * LANES : part + (b + 1) * LANES] = jnp.dot(
                notes, shift, preferred_element_type=f32
            ).astype(bf16)


def prepare(s, hidden, norm_gain, cache_length, expert_ids, expert_weight, width):
    requests, model_width = hidden.shape
    part = model_width // width
    blocks = -(-(1 + 4 * expert_ids.shape[1]) // NOTES)
    message = jax.ShapeDtypeStruct((requests, part + blocks * LANES), bf16)
    return pl.pallas_call(
        functools.partial(prepare_kernel, width),
        in_specs=[smem] + [vmem] * 5,
        out_specs=[vmem] * width,
        out_shape=[message] * width,
        scratch_shapes=[
            pltpu.VMEM((requests, model_width), bf16),
            pltpu.VMEM((blocks * NOTES, requests), f32),
        ],
        compiler_params=pltpu.CompilerParams(vmem_limit_bytes=56 * 2**20),
        cost_estimate=little,
    )(
        s.reshape(1),
        hidden,
        norm_gain.reshape(1, -1),
        cache_length.reshape(1, -1),
        expert_ids.T,
        expert_weight.T,
    )


def dispatch_kernel(senders, experts, top, requests, here_ref, *refs):
    messages, refs = refs[:senders], refs[senders:]
    outs, (map_ref, length_ref, tokens_ref, select_ref) = refs[:experts], refs[experts:]
    s, e = here_ref[0], here_ref[1]
    part = tokens_ref.shape[1]
    total = senders * requests
    room = senders * CAP_E
    for i in range(senders):
        tokens_ref[i * requests : (i + 1) * requests, :] = messages[i][:, :part]
    notes = []
    for at in range(part, messages[0].shape[1], LANES):
        summed = messages[0][:, at : at + LANES].astype(f32)
        for i in range(1, senders):
            summed = summed + messages[i][:, at : at + LANES].astype(f32)
        notes.append(summed)
    length_ref[...] = notes[0][0:1, :].astype(jnp.int32)

    def note(k):
        at = k % NOTES
        return notes[k // NOTES][at : at + 1, :total]

    rows = max(8, experts)
    expert = (e ^ lax.broadcasted_iota(jnp.int32, (rows, total), 0)).astype(f32)
    hit = jnp.zeros((rows, total), f32)
    share = jnp.zeros((rows, total), f32)
    for t in range(top):
        same = note(1 + t) == expert
        weight = note(1 + top + t) + note(1 + 2 * top + t) + note(1 + 3 * top + t)
        hit = jnp.where(same, 1.0, hit)
        share = share + jnp.where(same, weight, 0.0)
    shift = requests.bit_length() - 1
    a = lax.broadcasted_iota(jnp.int32, (total, total), 0)
    b = lax.broadcasted_iota(jnp.int32, (total, total), 1)
    same_sender = lax.shift_right_logical(a, shift) == lax.shift_right_logical(b, shift)
    ahead = (same_sender & (a < b)).astype(bf16)
    rank = jnp.dot(hit.astype(bf16), ahead, preferred_element_type=f32).astype(jnp.int32)
    lane = lax.broadcasted_iota(jnp.int32, (1, total), 1)
    base = (lax.shift_right_logical(lane, shift) ^ (s & 1)) * CAP_E
    spot = lax.broadcasted_iota(jnp.int32, (room, total), 0)
    for n in range(experts):
        inside = (hit[n : n + 1, :] > 0.5) & (rank[n : n + 1, :] < CAP_E)
        chosen = jnp.where(inside, base + rank[n : n + 1, :], -1) == spot
        select_ref[n * room : (n + 1) * room, :] = jnp.where(chosen, 1.0, 0.0)
        map_ref[n * room : (n + 1) * room, :] = jnp.where(chosen, share[n : n + 1, :], 0.0)
    select = select_ref[...].astype(bf16)
    tile = 256 if part % 256 == 0 else LANES
    for at in range(0, part, tile):
        sent = jnp.dot(select, tokens_ref[:, at : at + tile], preferred_element_type=f32)
        for n in range(experts):
            outs[n][:, at : at + tile] = sent[n * room : (n + 1) * room, :].astype(bf16)


def dispatch(s, e, messages, part, experts, top):
    senders = len(messages)
    requests = messages[0].shape[0]
    room, total = senders * CAP_E, senders * requests
    *outs, weight_map, lengths = pl.pallas_call(
        functools.partial(dispatch_kernel, senders, experts, top, requests),
        in_specs=[smem] + [vmem] * senders,
        out_specs=[vmem] * (experts + 2),
        out_shape=[jax.ShapeDtypeStruct((room, part), bf16)] * experts
        + [
            jax.ShapeDtypeStruct((experts * room, total), f32),
            jax.ShapeDtypeStruct((1, LANES), jnp.int32),
        ],
        scratch_shapes=[
            pltpu.VMEM((total, part), bf16),
            pltpu.VMEM((experts * room, total), f32),
        ],
        compiler_params=pltpu.CompilerParams(vmem_limit_bytes=16 * 2**20),
        cost_estimate=little,
    )(jnp.stack([s, e]).astype(jnp.int32), *messages)
    return outs, weight_map, lengths[0, :total].reshape(senders, requests)


def hold_kernel(in_ref, out_ref):
    out_ref[...] = in_ref[...]


def hold(x):
    return pl.pallas_call(
        hold_kernel,
        in_specs=[vmem],
        out_specs=vmem,
        out_shape=jax.ShapeDtypeStruct(x.shape, x.dtype),
        compiler_params=pltpu.CompilerParams(vmem_limit_bytes=2 * 2**20),
        cost_estimate=little,
    )(x)


def attend_all(queries, caches, lengths):
    scores = [
        lax.dot_general(cache, query, (((0,), (0,)), ((), ())), preferred_element_type=f32)
        for query, cache in zip(queries, caches)
    ]
    probs = []
    for score, length in zip(scores, lengths):
        score = score * score_scale
        places = lax.broadcasted_iota(jnp.int32, score.shape, 0)
        score = jnp.where(places < length, score, -jnp.inf)
        raised = jnp.exp(score - jnp.max(score, axis=0, keepdims=True))
        share = raised * (1.0 / jnp.sum(raised, axis=0, keepdims=True))
        probs.append(share.astype(bf16).T)
    return [
        lax.dot_general(
            prob, cache[:LAT], (((1,), (1,)), ((), ())), preferred_element_type=f32
        ).astype(bf16)
        for prob, cache in zip(probs, caches)
    ]


def attend_cost(count, heads, positions, width):
    return pl.CostEstimate(
        flops=2 * count * heads * positions * (width + LAT),
        bytes_accessed=count * 2 * (heads * width + positions * width + heads * LAT),
        transcendentals=count * heads * positions,
    )


def kept_kernel(step, length_ref, q_ref, c_ref, out_ref):
    i = pl.program_id(0)
    outs = attend_all(
        [q_ref[j] for j in range(step)],
        [c_ref[j] for j in range(step)],
        [length_ref[i * step + j] for j in range(step)],
    )
    for j in range(step):
        out_ref[j] = outs[j]


def attend_kept(queries, cache, lengths):
    count, width, heads = queries.shape
    positions = cache.shape[2]
    step = next(k for k in (8, 4, 2, 1) if count % k == 0)
    return pl.pallas_call(
        functools.partial(kept_kernel, step),
        grid_spec=pltpu.PrefetchScalarGridSpec(
            num_scalar_prefetch=1,
            grid=(count // step,),
            in_specs=[
                pl.BlockSpec((step, width, heads), lambda i, n: (i, 0, 0)),
                pl.BlockSpec((step, width, positions), lambda i, n: (i, 0, 0)),
            ],
            out_specs=pl.BlockSpec((step, heads, LAT), lambda i, n: (i, 0, 0)),
        ),
        out_shape=jax.ShapeDtypeStruct((count, heads, LAT), bf16),
        compiler_params=pltpu.CompilerParams(vmem_limit_bytes=ATTEND_VMEM),
        cost_estimate=attend_cost(count, heads, positions, width),
    )(lengths, queries, cache)


def lent_kernel(lent, index_ref, length_ref, *refs):
    outs = attend_all(
        [refs[i][0] for i in range(lent)],
        [refs[lent + i][0] for i in range(lent)],
        [length_ref[i] for i in range(lent)],
    )
    for i in range(lent):
        refs[2 * lent + i][...] = outs[i]


def attend_lent(queries, cache, index, lengths):
    lent = index.shape[0]
    _, width, heads = queries.shape
    positions = cache.shape[2]

    def at(i):
        return lambda step, idx, n: (idx[i], 0, 0)

    return pl.pallas_call(
        functools.partial(lent_kernel, lent),
        grid_spec=pltpu.PrefetchScalarGridSpec(
            num_scalar_prefetch=2,
            grid=(1,),
            in_specs=[pl.BlockSpec((1, width, heads), at(i)) for i in range(lent)]
            + [pl.BlockSpec((1, width, positions), at(i)) for i in range(lent)],
            out_specs=[pl.BlockSpec((heads, LAT), lambda step, idx, n: (0, 0))] * lent,
        ),
        out_shape=[jax.ShapeDtypeStruct((heads, LAT), bf16)] * lent,
        compiler_params=pltpu.CompilerParams(vmem_limit_bytes=ATTEND_VMEM),
        cost_estimate=attend_cost(lent, heads, positions, width),
    )(index, lengths, *[queries] * lent, *[cache] * lent)


def place_kernel(lent, where_ref, *refs):
    out_ref, sems = refs[lent + 1], refs[lent + 2]
    copies = [
        pltpu.make_async_copy(refs[i], out_ref.at[where_ref[i]], sems.at[i]) for i in range(lent)
    ]
    for copy in copies:
        copy.start()
    for copy in copies:
        copy.wait()


def place(where, taken, kept):
    lent = len(taken)
    return pl.pallas_call(
        functools.partial(place_kernel, lent),
        in_specs=[smem] + [pl.BlockSpec(memory_space=pl.ANY)] * lent + [hbm],
        out_specs=hbm,
        out_shape=jax.ShapeDtypeStruct(kept.shape, kept.dtype),
        scratch_shapes=[pltpu.SemaphoreType.DMA((lent,))],
        input_output_aliases={lent + 1: 0},
        compiler_params=pltpu.CompilerParams(vmem_limit_bytes=2 * 2**20),
    )(where, *taken, kept)


def total_sum(total, width, first):
    step = 2
    while step < width:
        got = xor_permute(total, "steal", step)
        if first is not None:
            got, first = lax.optimization_barrier((got, first))
        total = (total.astype(f32) + got.astype(f32)).astype(bf16)
        step *= 2
    return total, first


def per_device(
    queries,
    latent_cache,
    cache_length,
    steal_source,
    hidden,
    norm_gain,
    expert_ids,
    expert_weight,
    w_gate,
    w_up,
    w_down,
):
    s, e = lax.axis_index("steal"), lax.axis_index("ep")
    width, experts = lax.axis_size("steal"), lax.axis_size("ep")
    requests, model_width = hidden.shape
    top = expert_ids.shape[1]
    part = model_width // width
    core = s % 2
    lent = width - 1

    messages = prepare(s, hidden, norm_gain, cache_length, expert_ids, expert_weight, width)
    messages = [hold(messages[0])] + [xor_permute(messages[m], "steal", m) for m in range(1, width)]
    outgoing, weight_map, peer_lengths = dispatch(s, e, messages, part, experts, top)
    outgoing, peer_lengths = lax.optimization_barrier((outgoing, peer_lengths))
    pieces = [outgoing[0]] + [xor_permute(outgoing[n], "ep", n) for n in range(1, experts)]

    slot_ids = jnp.arange(lent, dtype=jnp.int32)
    others = jnp.arange(1, width, dtype=jnp.int32)[:, None]
    peer_lengths = peer_lengths[1:, :lent]
    partner = s ^ ((2 * s - steal_source[:lent]) % width)
    is_partner = partner[None, :] == others
    order = jnp.sum(jnp.where(is_partner, slot_ids[None, :], 0), axis=1)
    lent_lengths = jnp.sum(jnp.where(is_partner, peer_lengths, 0), axis=1)
    comes_from = (s ^ steal_source[:lent])[None, :] == others
    where = jnp.sum(jnp.where(comes_from, slot_ids[None, :], 0), axis=1)
    queries, cache = queries.swapaxes(1, 2), latent_cache.swapaxes(1, 2)
    given = attend_lent(queries, cache, order, lent_lengths)
    lengths, given = lax.optimization_barrier((cache_length, given))
    taken = [xor_permute(given[m - 1], "steal", m) for m in range(1, width)]
    kept = attend_kept(queries, cache, lengths)
    pieces, kept = lax.optimization_barrier((pieces, kept))

    half = w_gate.shape[2] // 2
    gate_send = lax.dynamic_slice(w_gate[0], (0, (1 - core) * half), (part, half))
    gate_keep = lax.dynamic_slice(w_gate[0], (0, core * half), (part, half))
    up_send = lax.dynamic_slice(w_up[0], (0, (1 - core) * half), (part, half))
    up_keep = lax.dynamic_slice(w_up[0], (0, core * half), (part, half))
    down_own = lax.dynamic_slice(w_down[0], (core * half, 0), (half, part))
    down_other = lax.dynamic_slice(w_down[0], ((1 - core) * half, 0), (half, part))

    chips, chip = width // CORES, s // CORES
    room = CORES * CAP_E
    arrived = [
        jnp.concatenate([pieces[n][j * room : (j + 1) * room] for n in range(experts)], axis=0)
        for j in range(chips)
    ]
    by_distance = jnp.stack(arrived)
    results = []
    total_before, produced_before = None, None
    for chunk in range(chips):
        arrived = lax.dynamic_index_in_dim(by_distance, chip ^ chunk, 0, keepdims=False)
        if chunk > 0:
            arrived, total_before = lax.optimization_barrier((arrived, total_before))
        send = jnp.concatenate(
            [
                jnp.dot(arrived, gate_send, preferred_element_type=f32).astype(bf16),
                jnp.dot(arrived, up_send, preferred_element_type=f32).astype(bf16),
            ],
            axis=1,
        )
        got = xor_permute(send, "steal", 1)
        keep = jnp.concatenate(
            [
                jnp.dot(arrived, gate_keep, preferred_element_type=f32),
                jnp.dot(arrived, up_keep, preferred_element_type=f32),
            ],
            axis=1,
        )
        total = (keep + got.astype(f32)).astype(bf16)
        if chunk == 0:
            total, taken = lax.optimization_barrier((total, taken))
        total_before = total
        total, produced_before = total_sum(total, width, produced_before)
        if chunk == 0:
            attended = place(where, taken, kept)
            total, attended = lax.optimization_barrier((total, attended))
        total = total.astype(f32)
        active = (jax.nn.silu(total[:, :half]) * total[:, half:]).astype(bf16)
        other = xor_permute(active, "steal", 1)
        produced = (
            jnp.dot(active, down_own, preferred_element_type=f32)
            + jnp.dot(other, down_other, preferred_element_type=f32)
        ).astype(bf16)
        produced_before = produced
        results.append(produced.reshape(experts, room, part))

    results = jnp.stack(results)
    back = [lax.dynamic_index_in_dim(results, chip ^ j, 0, keepdims=False) for j in range(chips)]
    far = jnp.concatenate(back[1:], axis=1)
    near = back[0]
    far_rows = far.shape[1]
    both = xor_permute(jnp.concatenate([far[1], near[1]], axis=0), "ep", 1)
    far = [far[0], both[:far_rows]] + [xor_permute(far[n], "ep", n) for n in range(2, experts)]
    near = [near[0], both[far_rows:]] + [xor_permute(near[n], "ep", n) for n in range(2, experts)]

    def mix(weight_map, returned):
        returned = jnp.concatenate(returned, axis=0).astype(f32)
        mixed = jnp.einsum(
            "ir,ik->rk",
            weight_map,
            returned,
            precision=lax.Precision.HIGHEST,
            preferred_element_type=f32,
        )
        return mixed.astype(bf16).reshape(-1, requests, part)

    weight_map = weight_map.reshape(experts, width * CAP_E, width * requests)
    split = CORES * requests
    mixed = mix(weight_map[:, room:, split:].reshape(-1, width * requests - split), far)
    got = [xor_permute(mixed[m - CORES], "steal", m) for m in range(CORES, width)]
    near, got = lax.optimization_barrier((near, got))
    mixed = mix(weight_map[:, :room, :split].reshape(-1, split), near)
    got = [mixed[0], xor_permute(mixed[1], "steal", 1)] + got
    result = jnp.zeros((requests, model_width), bf16)
    for m in range(width):
        result = lax.dynamic_update_slice(result, got[m], (0, (s ^ m) * part))
    return (attended, result)


def solution(mesh):
    return jax.shard_map(
        per_device,
        mesh=mesh,
        in_specs=(
            P(("rep", "steal", "ep"), None, None),
            P(("rep", "steal", "ep"), None, None),
            P(("rep", "steal", "ep")),
            P(("rep", "steal", "ep")),
            P(("rep", "steal", "ep"), None),
            P(),
            P(("rep", "steal", "ep"), None),
            P(("rep", "steal", "ep"), None),
            P("ep", "steal", None),
            P("ep", "steal", None),
            P("ep", None, "steal"),
        ),
        out_specs=(P(("rep", "steal", "ep"), None, None), P(("rep", "steal", "ep"), None)),
        check_vma=False,
    )
```
